512 devices in a mesh: rep: 64 (over z, y_hi, core), fsdp: 8 (over x, y_lo).
Axes of the slice: x: 4, y: 8 (y_hi: 4, y_lo: 2; y = y_hi * 2 + y_lo), z: 8, core: 2. Of those that a mesh axis runs over, the one named last changes fastest.
Arguments:
- hidden: bfloat16 [2, 65536, 4096], P(None, ('rep', 'fsdp')), may hold values from -6 to 6
- cotangent: bfloat16 [2, 65536, 512], P(None, ('rep', 'fsdp')), may hold values from -6 to 6
- local_weight: bfloat16 [64, 512, 4096], P('rep', None, 'fsdp'), may hold values from -16 to 16
- first_moment: bfloat16 [64, 512, 4096], P('rep', None, 'fsdp'), may hold values from -1.5 to 1.5
- second_moment: bfloat16 [64, 512, 4096], P('rep', None, 'fsdp'), may hold values from 0.0099487305 to 0.29882812
- global_weight: float32 [512, 4096], P('rep', 'fsdp'), may hold values from -6 to 6
- outer_momentum: float32 [512, 4096], P('rep', 'fsdp'), may hold values from -4 to 4
- step_count: int32 [1], replicated, may hold values from 1 to 5
Outputs:
- projected_keys: bfloat16 [2, 65536, 512], P(None, ('rep', 'fsdp'))
- final_weight: bfloat16 [64, 512, 4096], P('rep', None, 'fsdp')
- new_global: float32 [512, 4096], P('rep', 'fsdp')
- new_momentum: float32 [512, 4096], P('rep', 'fsdp')
The draws below stay inside these ranges and needn't reach their ends.
All inputs are finite; a program needn't handle non-finite values.
Results may differ from the reference program's by a relative error of at most 0.001.
The reference program's roundings to bfloat16 on the way (of `weight_bf`) count: a program that leaves them out, or rounds other values in their place, can miss the bound.
Values may be sent and summed in bfloat16 or wider, within the bound.
No kernel may reach another device: no remote copies, remote signals or barrier semaphores. Data moves between devices by JAX's collectives and lax.ppermute only.
A program may use at most 64 MiB of HBM per device.

```python
import math
import jax
import jax.numpy as jnp
from jax import lax

D = 4096
KVW = 512
STEPS = 2
REPLICAS = 64
TOKENS = 65536


def spiked(entries, rng, source, target, parts, factor):
    def block_of(dim):
        return (jnp.arange(entries.shape[dim]) // (entries.shape[dim] // parts)).reshape((-1,) + (1,) * (entries.ndim - 1 - dim))

    near = jax.random.permutation(rng, parts)[block_of(target)]
    other_side = (block_of(target) + parts // 2) % parts
    return jnp.where((block_of(source) == near) | (block_of(source) == other_side), factor * entries, entries)


def steps_of(key, dims, pieces, least, high):
    factor_of = 1.0
    for axis_at, shards_of in pieces:
        draws = jax.random.uniform(jax.random.fold_in(jax.random.fold_in(key, 6), axis_at), (shards_of,), jnp.float32, least / len(pieces), high / len(pieces))
        factor_of = factor_of * jnp.repeat(jnp.exp(draws), dims[axis_at] // shards_of).reshape((-1,) + (1,) * (len(dims) - 1 - axis_at))
    return factor_of


def noise(stream_key, shape, spread, most, pieces=(), dtype=jnp.bfloat16):
    result = jax.random.normal(stream_key, shape, jnp.float32) * spread
    if len(pieces) > 0:
        result = steps_of(stream_key, shape, pieces, -0.22, 0.18) * result
    return jnp.clip(result, min=-most, max=most).astype(dtype)


def gaussian_with(stream_key, extent, deviation, limit, pieces, heavy, kind=jnp.bfloat16):
    entries = deviation * jax.random.normal(stream_key, extent, jnp.float32)
    if pieces:
        entries = entries * steps_of(stream_key, extent, pieces, -0.22, 0.18)
    return jnp.clip(spiked(entries, jax.random.fold_in(stream_key, 3), *heavy), -limit, limit).astype(kind)


def setup_inputs(seed: int = 0) -> dict:
    keys = jax.random.split(jax.random.key(seed), 9)
    hidden = noise(keys[0], (STEPS, TOKENS, D), 1.0, 6.0, ((1, 512),))
    cotangent = noise(keys[1], (STEPS, TOKENS, KVW), 1.0, 6.0, ((1, 512),))
    local_weight = gaussian_with(keys[2], (REPLICAS, KVW, D), 1.0, 16.0, ((0, 64), (2, 8)), (0, 1, 64, 4.0))
    first_moment = noise(keys[3], (REPLICAS, KVW, D), 0.1, 1.5, ((0, 64), (2, 8)))
    second_moment = jnp.clip(jnp.exp(math.log(0.29882812) - 3.4024236 * jax.random.uniform(keys[4], (REPLICAS, KVW, D), jnp.float32) ** steps_of(keys[4], (REPLICAS, KVW, D), ((0, 64), (2, 8)), -0.2, 0.2)), 0.0099487305, 0.29882812).astype(jnp.bfloat16)
    global_weight = noise(keys[5], (KVW, D), 1.0, 6.0, ((0, 64), (1, 8)), jnp.float32)
    outer_momentum = noise(keys[6], (KVW, D), 0.3, 4.0, ((0, 64), (1, 8)), jnp.float32)
    step_count = jax.random.randint(keys[7], (1,), 1, 6).astype(jnp.int32)
    return {"hidden": hidden, "cotangent": cotangent, "local_weight": local_weight, "first_moment": first_moment, "second_moment": second_moment, "global_weight": global_weight, "outer_momentum": outer_momentum, "step_count": step_count}


def replica_steps(packed, new_global, first_count):
    features, upstream, weight, moment_one, moment_two = packed
    factor = D ** (-0.5)
    weight = weight.astype(jnp.float32)
    moment_one = moment_one.astype(jnp.float32)
    moment_two = moment_two.astype(jnp.float32)
    key_list = []
    for inner in range(STEPS):
        weight_bf = weight.astype(jnp.bfloat16)
        key_rows = jnp.dot(features[inner], weight_bf.T, preferred_element_type=jnp.float32) * factor
        key_list.append(key_rows.astype(jnp.bfloat16))
        gradient = jnp.dot(upstream[inner].T, features[inner], preferred_element_type=jnp.float32) * factor
        moment_one = 0.9 * moment_one + 0.1 * gradient
        moment_two = 0.95 * moment_two + 0.05 * gradient * gradient
        counter = first_count + (inner + 1)
        bias_one = 1.0 - jnp.power(0.9, counter)
        bias_two = 1.0 - jnp.power(0.95, counter)
        weight = weight - 0.05 * (moment_one / bias_one / (jnp.sqrt(moment_two / bias_two) + 1e-08) + 0.1 * weight)
        if inner == 0:
            weight = 0.5 * weight + 0.5 * new_global
    return (jnp.stack(key_list), weight.astype(jnp.bfloat16))

def reference(hidden, cotangent, local_weight, first_moment, second_moment, global_weight, outer_momentum, step_count):
    mean_local = lax.optimization_barrier(jnp.mean(local_weight.astype(jnp.float32), axis=0))
    difference = global_weight - mean_local
    new_momentum = 0.9 * outer_momentum + difference
    new_global = global_weight - 0.7 * (difference + 0.9 * new_momentum)
    per_rows = TOKENS // REPLICAS
    features = hidden.reshape(STEPS, REPLICAS, per_rows, D).transpose(1, 0, 2, 3)
    upstream = cotangent.reshape(STEPS, REPLICAS, per_rows, KVW).transpose(1, 0, 2, 3)
    first_count = step_count[0].astype(jnp.float32)
    key_rows, final_weight = lax.map(lambda packed: replica_steps(packed, new_global, first_count), (features, upstream, local_weight, first_moment, second_moment))
    projected_keys = key_rows.transpose(1, 0, 2, 3).reshape(STEPS, TOKENS, KVW)
    return (projected_keys, final_weight, new_global, new_momentum)
```

```python
import jax
import jax.numpy as jnp
from jax import lax
from jax.sharding import Mesh, PartitionSpec as P

D = 4096
STEPS = 2
REP = ("z", "y_hi", "core")
COLUMN = ("z", "y_hi")
FSDP = ("x", "y_lo")


def outer_update(local_weight, global_weight, outer_momentum):
    replicas = lax.axis_size(REP)
    rows, width = global_weight.shape
    shares = lax.all_to_all(
        local_weight[0].reshape(replicas, rows, width), REP, 0, 0, tiled=True
    )
    mean_local = jnp.sum(shares.astype(jnp.float32), axis=0) / replicas
    difference = global_weight - mean_local
    momentum = 0.9 * outer_momentum + difference
    updated = global_weight - 0.7 * (difference + 0.9 * momentum)
    columns = lax.axis_size(COLUMN)
    mine = lax.all_to_all(
        jnp.broadcast_to(updated, (columns, rows, width)), COLUMN, 0, 0, tiled=True
    )
    other = lax.ppermute(mine, "core", [(0, 1), (1, 0)])
    first = lax.axis_index("core") == 0
    landed = jnp.stack(
        [jnp.where(first, mine, other), jnp.where(first, other, mine)], axis=1
    ).reshape(replicas * rows, width)
    return (updated, momentum, landed)


def keys_by_exchange(product):
    parts = lax.axis_size(FSDP)
    rows, width = product.shape
    pieces = lax.all_to_all(
        product.reshape(parts, rows // parts, width), FSDP, 0, 0, tiled=True
    )
    return jnp.sum(pieces, axis=0)


def per_device(
    hidden,
    cotangent,
    local_weight,
    first_moment,
    second_moment,
    global_weight,
    outer_momentum,
    step_count,
):
    factor = D ** (-0.5)
    parts = lax.axis_size(FSDP)
    tokens = hidden.shape[1]
    width = hidden.shape[2] // parts
    cotangents = lax.all_gather(cotangent, FSDP, axis=1, tiled=True)
    updated, momentum, landed = outer_update(local_weight, global_weight, outer_momentum)
    by_owner = hidden.reshape(STEPS, tokens, parts, width).transpose(2, 0, 1, 3)
    columns = lax.all_to_all(by_owner, FSDP, 0, 0, tiled=True)
    weight = local_weight[0].astype(jnp.float32)
    moment_one = first_moment[0].astype(jnp.float32)
    moment_two = second_moment[0].astype(jnp.float32)
    first_count = step_count[0].astype(jnp.float32)
    key_list = []
    for inner in range(STEPS):
        weight_bf = weight.astype(jnp.bfloat16)
        step_columns = columns[:, inner].reshape(parts * tokens, width)
        step_upstream = cotangents[inner]
        product = lax.dot_general(
            step_columns, weight_bf, (((1,), (1,)), ((), ())), preferred_element_type=jnp.float32
        )
        if inner == 0:
            key_rows = lax.psum_scatter(product, FSDP, scatter_dimension=0, tiled=True)
        else:
            key_rows = keys_by_exchange(product)
        key_list.append((key_rows * factor).astype(jnp.bfloat16))
        gradient = (
            lax.dot_general(
                step_upstream,
                step_columns,
                (((0,), (0,)), ((), ())),
                preferred_element_type=jnp.float32,
            )
            * factor
        )
        moment_one = 0.9 * moment_one + 0.1 * gradient
        moment_two = 0.95 * moment_two + 0.05 * gradient * gradient
        counter = first_count + (inner + 1)
        bias_one = 1.0 - jnp.power(0.9, counter)
        bias_two = 1.0 - jnp.power(0.95, counter)
        weight = weight - 0.05 * (
            moment_one / bias_one / (jnp.sqrt(moment_two / bias_two) + 1e-08) + 0.1 * weight
        )
        if inner == 0:
            weight = 0.5 * weight + 0.5 * landed
    projected_keys = jnp.stack(key_list)
    final_weight = weight.astype(jnp.bfloat16)[None]
    return (projected_keys, final_weight, updated, momentum)


def solution(mesh):
    chips = Mesh(mesh.devices.reshape(8, 4, 2, 4, 2), REP + FSDP)
    tokens = P(None, REP + FSDP, None)
    replica = P(REP, None, FSDP)
    outer = P(REP, FSDP)
    return jax.shard_map(
        per_device,
        mesh=chips,
        in_specs=(tokens, tokens, replica, replica, replica, outer, outer, P()),
        out_specs=(tokens, replica, outer, outer),
        check_vma=False,
    )
```

```python
import jax
import jax.numpy as jnp
from jax import lax
from jax.sharding import Mesh, PartitionSpec as P

D = 4096
STEPS = 2
REP = ("z", "y_hi", "core")
COLUMN = ("z", "y_hi")
FSDP = ("x", "y_lo")


def swap(value, axis, mask):
    return lax.ppermute(value, axis, [(i, i ^ mask) for i in range(lax.axis_size(axis))])


def outer_update(local_weight, global_weight, outer_momentum):
    replicas = lax.axis_size(REP)
    rows, width = global_weight.shape
    shares = lax.all_to_all(
        local_weight[0].reshape(replicas, rows, width), REP, 0, 0, tiled=True
    )
    mean_local = jnp.sum(shares.astype(jnp.float32), axis=0) / replicas
    difference = global_weight - mean_local
    momentum = 0.9 * outer_momentum + difference
    updated = global_weight - 0.7 * (difference + 0.9 * momentum)
    columns = lax.axis_size(COLUMN)
    mine = lax.all_to_all(
        jnp.broadcast_to(updated, (columns, rows, width)), COLUMN, 0, 0, tiled=True
    )
    other = swap(mine, "core", 1)
    first = lax.axis_index("core") == 0
    landed = jnp.stack(
        [jnp.where(first, mine, other), jnp.where(first, other, mine)], axis=1
    ).reshape(replicas * rows, width)
    return (updated, momentum, landed)


def features_by_slot(hidden):
    wide, near = lax.axis_size("x"), lax.axis_size("y_lo")
    width = hidden.shape[2] // (wide * near)
    slots = []
    for a in range(wide):
        for b in range(near):
            block = (lax.axis_index("x") ^ a) * near + (lax.axis_index("y_lo") ^ b)
            piece = lax.dynamic_slice_in_dim(hidden, block * width, width, 2)
            slots.append(lax.ppermute(piece, FSDP, [(i, i ^ (a * near + b)) for i in range(wide * near)]) if a + b else piece)
    return slots


def cotangents_by_slot(cotangent):
    pair = jnp.stack([cotangent, swap(cotangent, "y_lo", 1)], axis=1)
    slots = [pair] + [swap(pair, "x", a) for a in range(1, lax.axis_size("x"))]
    return jnp.concatenate(slots, axis=1)


def keys_from_slots(product):
    wide, near = lax.axis_size("x"), lax.axis_size("y_lo")
    rows, width = product.shape
    slots = product.reshape(wide, near, rows // (wide * near), width)
    total = slots[0]
    for a in range(1, wide):
        total = total + swap(slots[a], "x", a)
    return total[0] + swap(total[1], "y_lo", 1)


def per_device(
    hidden,
    cotangent,
    local_weight,
    first_moment,
    second_moment,
    global_weight,
    outer_momentum,
    step_count,
):
    factor = D ** (-0.5)
    pieces = features_by_slot(hidden)
    cotangents = cotangents_by_slot(cotangent)
    updated, momentum, landed = outer_update(local_weight, global_weight, outer_momentum)
    weight = local_weight[0].astype(jnp.float32)
    moment_one = first_moment[0].astype(jnp.float32)
    moment_two = second_moment[0].astype(jnp.float32)
    first_count = step_count[0].astype(jnp.float32)
    key_list = []
    for inner in range(STEPS):
        weight_bf = weight.astype(jnp.bfloat16)
        step_columns = jnp.concatenate([piece[inner] for piece in pieces], axis=0)
        step_upstream = cotangents[inner].reshape(step_columns.shape[0], -1)
        product = lax.dot_general(
            step_columns, weight_bf, (((1,), (1,)), ((), ())), preferred_element_type=jnp.float32
        )
        key_rows = keys_from_slots(product)
        key_list.append((key_rows * factor).astype(jnp.bfloat16))
        gradient = (
            lax.dot_general(
                step_upstream,
                step_columns,
                (((0,), (0,)), ((), ())),
                preferred_element_type=jnp.float32,
            )
            * factor
        )
        moment_one = 0.9 * moment_one + 0.1 * gradient
        moment_two = 0.95 * moment_two + 0.05 * gradient * gradient
        counter = first_count + (inner + 1)
        bias_one = 1.0 - jnp.power(0.9, counter)
        bias_two = 1.0 - jnp.power(0.95, counter)
        weight = weight - 0.05 * (
            moment_one / bias_one / (jnp.sqrt(moment_two / bias_two) + 1e-08) + 0.1 * weight
        )
        if inner == 0:
            weight = 0.5 * weight + 0.5 * landed
    projected_keys = jnp.stack(key_list)
    final_weight = weight.astype(jnp.bfloat16)[None]
    return (projected_keys, final_weight, updated, momentum)


def solution(mesh):
    chips = Mesh(mesh.devices.reshape(8, 4, 2, 4, 2), REP + FSDP)
    tokens = P(None, REP + FSDP, None)
    replica = P(REP, None, FSDP)
    outer = P(REP, FSDP)
    return jax.shard_map(
        per_device,
        mesh=chips,
        in_specs=(tokens, tokens, replica, replica, replica, outer, outer, P()),
        out_specs=(tokens, replica, outer, outer),
        check_vma=False,
    )
```

```python
import jax
import jax.numpy as jnp
from jax import lax
from jax.sharding import Mesh, PartitionSpec as P

D = 4096
STEPS = 2
REP = ("z", "y_hi", "core")
COLUMN = ("z", "y_hi")
FSDP = ("x", "y_lo")


def swap(value, axis, mask):
    return lax.ppermute(value, axis, [(i, i ^ mask) for i in range(lax.axis_size(axis))])


def outer_update(local_weight, global_weight, outer_momentum):
    replicas = lax.axis_size(REP)
    rows, width = global_weight.shape
    shares = lax.all_to_all(
        local_weight[0].reshape(replicas, rows, width), REP, 0, 0, tiled=True
    )
    mean_local = jnp.sum(shares.astype(jnp.float32), axis=0) / replicas
    difference = global_weight - mean_local
    momentum = 0.9 * outer_momentum + difference
    updated = global_weight - 0.7 * (difference + 0.9 * momentum)
    columns = lax.axis_size(COLUMN)
    mine = lax.all_to_all(
        jnp.broadcast_to(updated, (columns, rows, width)), COLUMN, 0, 0, tiled=True
    )
    other = swap(mine, "core", 1)
    first = lax.axis_index("core") == 0
    landed = jnp.stack(
        [jnp.where(first, mine, other), jnp.where(first, other, mine)], axis=1
    ).reshape(replicas * rows, width)
    return (updated, momentum, landed)


def features_by_slot(hidden, cotangent):
    wide, near = lax.axis_size("x"), lax.axis_size("y_lo")
    width = hidden.shape[2] // (wide * near)
    slots = jnp.zeros((wide * near,) + hidden.shape[:2] + (width,), hidden.dtype)
    place = lax.axis_index(FSDP)
    for k in range(wide * near):
        piece = lax.dynamic_slice_in_dim(hidden, (place ^ k) * width, width, 2)
        if k == 1:
            piece = jnp.concatenate([piece, cotangent])
        landed = swap(piece, FSDP, k) if k else piece
        if k == 1:
            landed, near_cotangent = landed[: hidden.shape[0]], landed[hidden.shape[0] :]
        slots = slots.at[k].set(landed)
    pair = jnp.stack([cotangent, near_cotangent], axis=1)
    pairs = [pair] + [swap(pair, "x", a) for a in range(1, wide)]
    return slots, jnp.concatenate(pairs, axis=1)


def keys_from_slots(product):
    wide, near = lax.axis_size("x"), lax.axis_size("y_lo")
    rows, width = product.shape
    slots = product.reshape(wide, near, rows // (wide * near), width)
    total = slots[0]
    for a in range(1, wide):
        total = total + swap(slots[a], "x", a)
    return total[0] + swap(total[1], "y_lo", 1)


def per_device(
    hidden,
    cotangent,
    local_weight,
    first_moment,
    second_moment,
    global_weight,
    outer_momentum,
    step_count,
):
    factor = D ** (-0.5)
    pieces, cotangents = features_by_slot(hidden, cotangent)
    updated, momentum, landed = outer_update(local_weight, global_weight, outer_momentum)
    weight = local_weight[0].astype(jnp.float32)
    moment_one = first_moment[0].astype(jnp.float32)
    moment_two = second_moment[0].astype(jnp.float32)
    first_count = step_count[0].astype(jnp.float32)
    key_list = []
    for inner in range(STEPS):
        weight_bf = weight.astype(jnp.bfloat16)
        step_columns = pieces[:, inner].reshape(-1, pieces.shape[3])
        step_upstream = cotangents[inner].reshape(step_columns.shape[0], -1)
        product = lax.dot_general(
            step_columns, weight_bf, (((1,), (1,)), ((), ())), preferred_element_type=jnp.float32
        )
        key_rows = keys_from_slots(product)
        key_list.append((key_rows * factor).astype(jnp.bfloat16))
        gradient = (
            lax.dot_general(
                step_upstream,
                step_columns,
                (((0,), (0,)), ((), ())),
                preferred_element_type=jnp.float32,
            )
            * factor
        )
        moment_one = 0.9 * moment_one + 0.1 * gradient
        moment_two = 0.95 * moment_two + 0.05 * gradient * gradient
        counter = first_count + (inner + 1)
        bias_one = 1.0 - jnp.power(0.9, counter)
        bias_two = 1.0 - jnp.power(0.95, counter)
        weight = weight - 0.05 * (
            moment_one / bias_one / (jnp.sqrt(moment_two / bias_two) + 1e-08) + 0.1 * weight
        )
        if inner == 0:
            weight = 0.5 * weight + 0.5 * landed
    projected_keys = jnp.stack(key_list)
    final_weight = weight.astype(jnp.bfloat16)[None]
    return (projected_keys, final_weight, updated, momentum)


def solution(mesh):
    chips = Mesh(mesh.devices.reshape(8, 4, 2, 4, 2), REP + FSDP)
    tokens = P(None, REP + FSDP, None)
    replica = P(REP, None, FSDP)
    outer = P(REP, FSDP)
    return jax.shard_map(
        per_device,
        mesh=chips,
        in_specs=(tokens, tokens, replica, replica, replica, outer, outer, P()),
        out_specs=(tokens, replica, outer, outer),
        check_vma=False,
    )
```
